256 devices in a mesh: energy: 64 (over z, y_lo, x), mom: 4 (over y_hi, core).
Axes of the slice: x: 4, y: 4 (y_hi: 2, y_lo: 2; y = y_hi * 2 + y_lo), z: 8, core: 2. Of those that a mesh axis runs over, the one named last changes fastest.
Arguments:
- green_lesser: bfloat16 [64, 4, 2, 512, 512], P('energy', 'mom'), may hold values from -6 to 6
- coupling: bfloat16 [4, 512, 512], replicated, may hold values from -0.25 to 0.25
- offsets: int32 [4], replicated, may hold values from 1 to 4, as said below
- occupation: float32 [4], replicated, may hold values from 0.05 to 2
- transfer_weight: float32 [4, 4], replicated, may hold values from 0.2 to 1
- transfer_table: int32 [4, 4], replicated, may hold values from 0 to 3, as said below
Outputs:
- sigma_lesser: bfloat16 [64, 4, 2, 512, 512], P('energy', 'mom')
The draws below stay inside these ranges and needn't reach their ends.
Inputs may be any that keep to these rules, and one draw needn't show every extreme that they name: The 4 offsets are distinct. `transfer_table`: each row names every momentum once.
All inputs are finite; a program needn't handle non-finite values.
Results may differ from the reference program's by a relative error of at most 0.0058.
Values may be sent and summed in bfloat16 or wider, within the bound.
No kernel may reach another device: no remote copies, remote signals or barrier semaphores. Data moves between devices by JAX's collectives and lax.ppermute only.
A program may use at most 64 MiB of HBM per device.

```python
import math
import jax
import jax.numpy as jnp
from jax import lax

NO = 512
NM = 4
MAXOFF = 4
K = 4
ENERGIES = 64


def draw_offsets(key, part):
    key = jax.random.fold_in(key, 11)
    order = jax.random.permutation(key, jnp.arange(MAXOFF, dtype=jnp.int32))
    return order[:NM] + 1


def draw_transfer_table(key, part):
    key = jax.random.fold_in(key, 23)
    scores = jax.random.randint(key, (K,), 0, 1 << 20, dtype=jnp.int32)
    scores = scores * K + jnp.arange(K, dtype=jnp.int32)
    perm = jnp.argsort(scores, stable=True).astype(jnp.int32)
    moment = jnp.arange(K, dtype=jnp.int32)
    return (moment[:, None] + perm[None, :]) % K


def block_scale(own_key, shape, shards, smallest, largest):
    level, own = 1.0, jax.random.fold_in(own_key, 6)
    for dim, shards_of in shards:
        heights = jnp.exp(jax.random.uniform(jax.random.fold_in(own, dim), (shards_of,), jnp.float32, smallest / len(shards), largest / len(shards)))
        level = level * jnp.repeat(heights, shape[dim] // shards_of).reshape([-1 if axis == dim else 1 for axis in range(len(shape))])
    return level


def normal_values(key, shape, scale, limit, shards=(), kind=jnp.bfloat16):
    gain = block_scale(key, shape, shards, -0.22, 0.18) if shards else 1.0
    array = jax.random.normal(key, shape, jnp.float32) * scale * gain
    return jnp.minimum(jnp.maximum(array, -limit), limit).astype(kind)


def setup_inputs(seed: int = 0) -> dict:
    streams_of = jax.random.split(jax.random.key(seed), 7)
    return {
        "green_lesser": normal_values(streams_of[0], (ENERGIES, K, 2, NO, NO), 1.0, 6.0, ((0, 64), (1, 4))),
        "coupling": normal_values(streams_of[1], (NM, NO, NO), NO ** -0.5, 0.25),
        "offsets": draw_offsets(jax.random.fold_in(streams_of[6], 71), 0),
        "occupation": jnp.clip(jnp.exp(jax.random.uniform(streams_of[3], (NM,), jnp.float32, math.log(0.05), math.log(2.0))), 0.05, 2.0),
        "transfer_weight": jnp.clip(jnp.exp(jax.random.uniform(streams_of[4], (K, NM), jnp.float32, math.log(0.2), math.log(1.0))), 0.2, 1.0),
        "transfer_table": draw_transfer_table(jax.random.fold_in(streams_of[6], 71), 0),
    }


def build_coef(offsets, occupation):
    steps = jnp.arange(1, MAXOFF + 1, dtype=jnp.int32)
    onehot = (offsets[:, None] == steps[None, :]).astype(jnp.float32)
    return jnp.concatenate([occupation[:, None] * onehot, (occupation[:, None] + 1.0) * onehot], axis=1)

def build_mixing(transfer_weight, transfer_table):
    count = transfer_table.shape[0]
    target = jnp.arange(count, dtype=jnp.int32)
    onehot = (transfer_table[:, :, None] == target[None, None, :]).astype(jnp.float32)
    return jnp.einsum('qv,kqj->vkj', transfer_weight, onehot, precision=lax.Precision.HIGHEST)

def reference(green_lesser, coupling, offsets, occupation, transfer_weight, transfer_table):
    coef = build_coef(offsets, occupation)
    mixing = build_mixing(transfer_weight, transfer_table)
    padded = jnp.pad(green_lesser, ((MAXOFF, MAXOFF), (0, 0), (0, 0), (0, 0), (0, 0)))
    coupling_wide = coupling.astype(jnp.float32)

    def one_energy(energy):
        picks = []
        for dist in range(1, MAXOFF + 1):
            picks.append(lax.dynamic_slice_in_dim(padded, (energy + MAXOFF - dist).astype(jnp.int32), 1, 0))
        for dist in range(1, MAXOFF + 1):
            picks.append(lax.dynamic_slice_in_dim(padded, (energy + MAXOFF + dist).astype(jnp.int32), 1, 0))
        stacked = jnp.concatenate(picks, axis=0).astype(jnp.float32)
        shifted = jnp.einsum('vc,ckpij->vkpij', coef, stacked, precision=lax.Precision.HIGHEST).astype(jnp.bfloat16)
        left = jnp.einsum('vij,vkpjl->vkpil', coupling_wide, shifted.astype(jnp.float32), precision=lax.Precision.HIGHEST).astype(jnp.bfloat16)
        term = jnp.einsum('vkpil,vml->vkpim', left.astype(jnp.float32), coupling_wide, precision=lax.Precision.HIGHEST)
        total = jnp.einsum('vkj,vjpim->kpim', mixing, term, precision=lax.Precision.HIGHEST)
        return total.astype(jnp.bfloat16)
    return lax.map(one_energy, jnp.arange(green_lesser.shape[0], dtype=jnp.int32))
```

```python
import functools
import jax
import jax.numpy as jnp
from jax import lax
from jax.experimental import pallas as pl
from jax.experimental.pallas import tpu as pltpu
from jax.sharding import Mesh, PartitionSpec as P

PLANES, ROWS, XS, HALVES, CORES = 8, 2, 4, 2, 2
PLANE = ("lo", "x", "hi", "core")
NE = ROWS * XS
NK = HALVES * CORES
NV = 4
NO = 512
SLICES = NE * NK
DEPTH = 2 * NO // SLICES
HALO = 4


def mix_kernel(offsets, occupation, weight, table, below, own, above, out, raw, mixing):
    raw[0:HALO] = below[...].reshape(HALO, NK, DEPTH, NO).astype(jnp.float32)
    raw[HALO : HALO + NE] = own[...].reshape(NE, NK, DEPTH, NO).astype(jnp.float32)
    raw[HALO + NE :] = above[...].reshape(HALO, NK, DEPTH, NO).astype(jnp.float32)
    for k in range(NK):
        for q in range(NK):
            for v in range(NV):
                mixing[v, k, table[k, q]] = weight[q, v]

    def step(index, carry):
        v = index // NE
        e = index % NE
        off = offsets[v]
        low = occupation[v]
        high = low + 1.0
        for part in range(DEPTH // 16):
            rows = slice(part * 16, part * 16 + 16)
            shifted = [
                low * raw[e + HALO - off, j, rows, :] + high * raw[e + HALO + off, j, rows, :]
                for j in range(NK)
            ]
            for k in range(NK):
                total = mixing[v, k, 0] * shifted[0]
                for j in range(1, NK):
                    total = total + mixing[v, k, j] * shifted[j]
                out[e * NK + k, v, rows, :] = total.astype(jnp.bfloat16)
        return carry

    lax.fori_loop(0, NV * NE, step, 0)


def mixed(offsets, occupation, weight, table, below, own, above):
    smem = pl.BlockSpec(memory_space=pltpu.SMEM)
    vmem = pl.BlockSpec(memory_space=pltpu.VMEM)
    return pl.pallas_call(
        mix_kernel,
        out_shape=jax.ShapeDtypeStruct((SLICES, NV, DEPTH, NO), jnp.bfloat16),
        in_specs=[smem] * 4 + [vmem] * 3,
        out_specs=vmem,
        scratch_shapes=[
            pltpu.VMEM((NE + 2 * HALO, NK, DEPTH, NO), jnp.float32),
            pltpu.SMEM((NV, NK, NK), jnp.float32),
        ],
        compiler_params=pltpu.CompilerParams(vmem_limit_bytes=24 << 20),
    )(offsets, occupation, weight, table, below, own, above)


def product_kernel(coupling, shifted, out):
    for part in range(2):
        total = None
        for v in range(NV):
            block = shifted[part * 16 : part * 16 + 16, v].reshape(NO, NO)
            left = jnp.dot(coupling[v], block, preferred_element_type=jnp.float32)
            term = lax.dot_general(
                left.astype(jnp.bfloat16),
                coupling[v],
                (((1,), (1,)), ((), ())),
                preferred_element_type=jnp.float32,
            )
            total = term if total is None else total + term
        out[part] = total.astype(jnp.bfloat16)


def products(coupling, shifted):
    vmem = pl.BlockSpec(memory_space=pltpu.VMEM)
    return pl.pallas_call(
        product_kernel,
        out_shape=jax.ShapeDtypeStruct((2, NO, NO), jnp.bfloat16),
        in_specs=[vmem] * 2,
        out_specs=vmem,
        compiler_params=pltpu.CompilerParams(vmem_limit_bytes=32 << 20),
    )(coupling, shifted)


def shards(green_lesser, coupling, offsets, occupation, transfer_weight, transfer_table):
    slices = green_lesser.reshape(SLICES, DEPTH, NO)
    own = lax.all_to_all(slices, PLANE, 0, 0, tiled=True)
    half = SLICES // 2
    below = lax.ppermute(own[half:], "z", [(z, z + 1) for z in range(PLANES - 1)])
    above = lax.ppermute(own[:half], "z", [(z + 1, z) for z in range(PLANES - 1)])
    out = mixed(offsets, occupation, transfer_weight, transfer_table, below, own, above)
    shifted = lax.all_to_all(out.reshape(SLICES, NV * DEPTH, NO), PLANE, 0, 0, tiled=True)
    sigma = products(coupling, shifted.reshape(SLICES, NV, DEPTH, NO))
    return sigma[None, None]


def solution(mesh):
    fine = Mesh(
        mesh.devices.reshape(PLANES, ROWS, XS, HALVES, CORES),
        ("z", "lo", "x", "hi", "core"),
    )
    split = P(("z", "lo", "x"), ("hi", "core"), None, None, None)
    return jax.shard_map(
        shards,
        mesh=fine,
        in_specs=(split, P(), P(), P(), P(), P()),
        out_specs=split,
        check_vma=False,
    )
```

```python
import jax
import jax.numpy as jnp
from jax import lax
from jax.experimental import pallas as pl
from jax.experimental.pallas import tpu as pltpu
from jax.sharding import Mesh, PartitionSpec as P

PLANES, ROWS, XS, HALVES, CORES = 8, 2, 4, 2, 2
PLANE = ("lo", "x", "hi", "core")
NE = ROWS * XS
NK = HALVES * CORES
NV = 4
NO = 512
SLICES = NE * NK
DEPTH = 2 * NO // SLICES
HALO = 4
WIDE = NK * DEPTH


def weight_kernel(offsets, occupation, weight, table, out, mixing):
    for k in range(NK):
        for q in range(NK):
            for v in range(NV):
                mixing[v, k, table[k, q]] = weight[q, v]
    row = lax.broadcasted_iota(jnp.int32, (DEPTH, WIDE), 0)
    column = lax.broadcasted_iota(jnp.int32, (DEPTH, WIDE), 1)
    for v in range(NV):
        for k in range(NK):
            base = jnp.zeros((DEPTH, WIDE), jnp.float32)
            for j in range(NK):
                base = jnp.where(column == row + DEPTH * j, mixing[v, k, j], base)
            for side in range(2):
                scaled = base * (occupation[v] + float(side))
                high = scaled.astype(jnp.bfloat16)
                rest = (scaled - high.astype(jnp.float32)).astype(jnp.bfloat16)
                columns = slice(side * WIDE, (side + 1) * WIDE)
                out[v, k * DEPTH : (k + 1) * DEPTH, columns] = high
                out[v, WIDE + k * DEPTH : WIDE + (k + 1) * DEPTH, columns] = rest


def mix(offsets, scale, out, sources, energies):
    for dist in range(1, HALO + 1):
        mode = jnp.int32(0)
        for v in range(1, NV):
            mode = jnp.where(offsets[v] == dist, v, mode)
        for e in energies(dist):
            pair = jnp.concatenate([sources(e - dist), sources(e + dist)], axis=0)
            total = jnp.dot(scale[mode], pair, preferred_element_type=jnp.float32)
            total = (total[:WIDE] + total[WIDE:]).astype(jnp.bfloat16)
            for k in range(NK):
                out[e * NK + k, mode] = total[k * DEPTH : (k + 1) * DEPTH]


def inner(dist):
    return range(dist, NE - dist)


def outer(dist):
    return [e for e in range(NE) if e not in inner(dist)]


def inner_kernel(offsets, scale, own, out):
    mix(offsets, scale, out, lambda e: own[e * NK : (e + 1) * NK].reshape(WIDE, NO), inner)


def outer_kernel(offsets, scale, own, below, above, started, out):
    def sources(e):
        ref, first = (below, e + HALO) if e < 0 else (own, e) if e < NE else (above, e - NE)
        return ref[first * NK : (first + 1) * NK].reshape(WIDE, NO)

    mix(offsets, scale, out, sources, outer)


SMEM = pl.BlockSpec(memory_space=pltpu.SMEM)
VMEM = pl.BlockSpec(memory_space=pltpu.VMEM)
MIXED = jax.ShapeDtypeStruct((SLICES, NV, DEPTH, NO), jnp.bfloat16)


def scales(offsets, occupation, weight, table):
    return pl.pallas_call(
        weight_kernel,
        out_shape=jax.ShapeDtypeStruct((NV, 2 * WIDE, 2 * WIDE), jnp.bfloat16),
        in_specs=[SMEM] * 4,
        out_specs=VMEM,
        scratch_shapes=[pltpu.SMEM((NV, NK, NK), jnp.float32)],
    )(offsets, occupation, weight, table)


def mixed_inner(offsets, scale, own):
    return pl.pallas_call(
        inner_kernel,
        out_shape=MIXED,
        in_specs=[SMEM, VMEM, VMEM],
        out_specs=VMEM,
        compiler_params=pltpu.CompilerParams(vmem_limit_bytes=24 << 20),
    )(offsets, scale, own)


def mixed_outer(offsets, scale, own, below, above, started):
    return pl.pallas_call(
        outer_kernel,
        out_shape=MIXED,
        in_specs=[SMEM] + [VMEM] * 5,
        out_specs=VMEM,
        input_output_aliases={5: 0},
        compiler_params=pltpu.CompilerParams(vmem_limit_bytes=24 << 20),
    )(offsets, scale, own, below, above, started)


def product_kernel(coupling, shifted, out):
    for part in range(2):
        total = None
        for v in range(NV):
            block = shifted[part * 16 : part * 16 + 16, v].reshape(NO, NO)
            left = jnp.dot(coupling[v], block, preferred_element_type=jnp.float32)
            term = lax.dot_general(
                left.astype(jnp.bfloat16),
                coupling[v],
                (((1,), (1,)), ((), ())),
                preferred_element_type=jnp.float32,
            )
            total = term if total is None else total + term
        out[part] = total.astype(jnp.bfloat16)


def products(coupling, shifted):
    vmem = pl.BlockSpec(memory_space=pltpu.VMEM)
    return pl.pallas_call(
        product_kernel,
        out_shape=jax.ShapeDtypeStruct((2, NO, NO), jnp.bfloat16),
        in_specs=[vmem] * 2,
        out_specs=vmem,
        compiler_params=pltpu.CompilerParams(vmem_limit_bytes=32 << 20),
    )(coupling, shifted)


def shards(green_lesser, coupling, offsets, occupation, transfer_weight, transfer_table):
    slices = green_lesser.reshape(SLICES, DEPTH, NO)
    own = lax.all_to_all(slices, PLANE, 0, 0, tiled=True)
    half = SLICES // 2
    below = lax.ppermute(own[half:], "z", [(z, z + 1) for z in range(PLANES - 1)])
    above = lax.ppermute(own[:half], "z", [(z + 1, z) for z in range(PLANES - 1)])
    scale = scales(offsets, occupation, transfer_weight, transfer_table)
    out = mixed_outer(offsets, scale, own, below, above, mixed_inner(offsets, scale, own))
    shifted = lax.all_to_all(out.reshape(SLICES, NV * DEPTH, NO), PLANE, 0, 0, tiled=True)
    sigma = products(coupling, shifted.reshape(SLICES, NV, DEPTH, NO))
    return sigma[None, None]


def solution(mesh):
    fine = Mesh(
        mesh.devices.reshape(PLANES, ROWS, XS, HALVES, CORES),
        ("z", "lo", "x", "hi", "core"),
    )
    split = P(("z", "lo", "x"), ("hi", "core"), None, None, None)
    return jax.shard_map(
        shards,
        mesh=fine,
        in_specs=(split, P(), P(), P(), P(), P()),
        out_specs=split,
        check_vma=False,
    )
```

```python
import jax
import jax.numpy as jnp
from jax import lax
from jax.experimental import pallas as pl
from jax.experimental.pallas import tpu as pltpu
from jax.sharding import Mesh, PartitionSpec as P

PLANES, ROWS, XS, HALVES, CORES = 8, 2, 4, 2, 2
PLANE = ("lo", "x", "hi", "core")
NE = ROWS * XS
NK = HALVES * CORES
NV = 4
NO = 512
SLICES = NE * NK
DEPTH = 2 * NO // SLICES
HALO = 4
WIDE = NK * DEPTH


def weight_kernel(offsets, occupation, weight, table, out, mixing):
    for k in range(NK):
        for q in range(NK):
            for v in range(NV):
                mixing[v, k, table[k, q]] = weight[q, v]
    row = lax.broadcasted_iota(jnp.int32, (DEPTH, WIDE), 0)
    column = lax.broadcasted_iota(jnp.int32, (DEPTH, WIDE), 1)
    for v in range(NV):
        for k in range(NK):
            base = jnp.zeros((DEPTH, WIDE), jnp.float32)
            for j in range(NK):
                base = jnp.where(column == row + DEPTH * j, mixing[v, k, j], base)
            for side in range(2):
                scaled = base * (occupation[v] + float(side))
                high = scaled.astype(jnp.bfloat16)
                rest = (scaled - high.astype(jnp.float32)).astype(jnp.bfloat16)
                rows = slice(k * DEPTH, (k + 1) * DEPTH)
                out[v, rows, 2 * side * WIDE : (2 * side + 1) * WIDE] = high
                out[v, rows, (2 * side + 1) * WIDE : (2 * side + 2) * WIDE] = rest


def mode_at(offsets, dist):
    mode = jnp.int32(0)
    for v in range(1, NV):
        mode = jnp.where(offsets[v] == dist, v, mode)
    return mode


LOW, HIGH = 0, 1
DISTS = range(1, HALO + 1)
PAIRS = [(dist, e) for dist in DISTS for e in range(NE)]
BELOW = [(dist, e) for dist, e in PAIRS if e < dist]
ABOVE = [(dist, e) for dist, e in PAIRS if e + dist >= NE]
INNER = [pair for pair in PAIRS if pair not in BELOW + ABOVE]


def block(ref, e):
    return ref[e * NK : (e + 1) * NK].reshape(WIDE, NO)


def one_side(scale, mode, side, source):
    weight = scale[mode, :, 2 * side * WIDE : (2 * side + 2) * WIDE]
    twice = jnp.concatenate([source, source], axis=0)
    return jnp.dot(weight, twice, preferred_element_type=jnp.float32)


def store(out, e, mode, total):
    rounded = total.astype(jnp.bfloat16)
    for k in range(NK):
        out[e * NK + k, mode] = rounded[k * DEPTH : (k + 1) * DEPTH]


def inner_kernel(offsets, scale, own, out, low_rest, high_rest):
    for dist, e in INNER:
        mode = mode_at(offsets, dist)
        low, high = block(own, e - dist), block(own, e + dist)
        both = jnp.concatenate([low, low, high, high], axis=0)
        store(out, e, mode, jnp.dot(scale[mode], both, preferred_element_type=jnp.float32))
    for index, (dist, e) in enumerate(BELOW):
        low_rest[index] = one_side(scale, mode_at(offsets, dist), HIGH, block(own, e + dist))
    for index, (dist, e) in enumerate(ABOVE):
        high_rest[index] = one_side(scale, mode_at(offsets, dist), LOW, block(own, e - dist))


def below_kernel(offsets, scale, below, rest, started, out):
    for index, (dist, e) in enumerate(BELOW):
        mode = mode_at(offsets, dist)
        term = one_side(scale, mode, LOW, block(below, e - dist + HALO))
        store(out, e, mode, rest[index] + term)


def above_kernel(offsets, scale, above, rest, started, out):
    for index, (dist, e) in enumerate(ABOVE):
        mode = mode_at(offsets, dist)
        term = one_side(scale, mode, HIGH, block(above, e + dist - NE))
        store(out, e, mode, rest[index] + term)


SMEM = pl.BlockSpec(memory_space=pltpu.SMEM)
VMEM = pl.BlockSpec(memory_space=pltpu.VMEM)
PARAMS = pltpu.CompilerParams(vmem_limit_bytes=32 << 20)
MIXED = jax.ShapeDtypeStruct((SLICES, NV, DEPTH, NO), jnp.bfloat16)


def scales(offsets, occupation, weight, table):
    return pl.pallas_call(
        weight_kernel,
        out_shape=jax.ShapeDtypeStruct((NV, WIDE, 4 * WIDE), jnp.bfloat16),
        in_specs=[SMEM] * 4,
        out_specs=VMEM,
        scratch_shapes=[pltpu.SMEM((NV, NK, NK), jnp.float32)],
    )(offsets, occupation, weight, table)


def mixed_inner(offsets, scale, own):
    rests = [jax.ShapeDtypeStruct((len(p), WIDE, NO), jnp.float32) for p in (BELOW, ABOVE)]
    return pl.pallas_call(
        inner_kernel,
        out_shape=[MIXED, *rests],
        in_specs=[SMEM, VMEM, VMEM],
        out_specs=[VMEM] * 3,
        compiler_params=PARAMS,
    )(offsets, scale, own)


def mixed_side(kernel, offsets, scale, halo, rest, started):
    return pl.pallas_call(
        kernel,
        out_shape=MIXED,
        in_specs=[SMEM] + [VMEM] * 4,
        out_specs=VMEM,
        input_output_aliases={4: 0},
        compiler_params=PARAMS,
    )(offsets, scale, halo, rest, started)


def product_kernel(coupling, shifted, out):
    for part in range(2):
        total = None
        for v in range(NV):
            block = shifted[part * 16 : part * 16 + 16, v].reshape(NO, NO)
            left = jnp.dot(coupling[v], block, preferred_element_type=jnp.float32)
            term = lax.dot_general(
                left.astype(jnp.bfloat16),
                coupling[v],
                (((1,), (1,)), ((), ())),
                preferred_element_type=jnp.float32,
            )
            total = term if total is None else total + term
        out[part] = total.astype(jnp.bfloat16)


def products(coupling, shifted):
    vmem = pl.BlockSpec(memory_space=pltpu.VMEM)
    return pl.pallas_call(
        product_kernel,
        out_shape=jax.ShapeDtypeStruct((2, NO, NO), jnp.bfloat16),
        in_specs=[vmem] * 2,
        out_specs=vmem,
        compiler_params=pltpu.CompilerParams(vmem_limit_bytes=32 << 20),
    )(coupling, shifted)


def shards(green_lesser, coupling, offsets, occupation, transfer_weight, transfer_table):
    slices = green_lesser.reshape(SLICES, DEPTH, NO)
    own = lax.all_to_all(slices, PLANE, 0, 0, tiled=True)
    half = SLICES // 2
    below = lax.ppermute(own[half:], "z", [(z, z + 1) for z in range(PLANES - 1)])
    above = lax.ppermute(own[:half], "z", [(z + 1, z) for z in range(PLANES - 1)])
    scale = scales(offsets, occupation, transfer_weight, transfer_table)
    out, low_rest, high_rest = mixed_inner(offsets, scale, own)
    out = mixed_side(above_kernel, offsets, scale, above, high_rest, out)
    out = mixed_side(below_kernel, offsets, scale, below, low_rest, out)
    shifted = lax.all_to_all(out.reshape(SLICES, NV * DEPTH, NO), PLANE, 0, 0, tiled=True)
    sigma = products(coupling, shifted.reshape(SLICES, NV, DEPTH, NO))
    return sigma[None, None]


def solution(mesh):
    fine = Mesh(
        mesh.devices.reshape(PLANES, ROWS, XS, HALVES, CORES),
        ("z", "lo", "x", "hi", "core"),
    )
    split = P(("z", "lo", "x"), ("hi", "core"), None, None, None)
    return jax.shard_map(
        shards,
        mesh=fine,
        in_specs=(split, P(), P(), P(), P(), P()),
        out_specs=split,
        check_vma=False,
    )
```

```python
import functools

import jax
import jax.numpy as jnp
from jax import lax
from jax.experimental import pallas as pl
from jax.experimental.pallas import tpu as pltpu
from jax.sharding import Mesh, PartitionSpec as P

PLANES, ROWS, XS, HALVES, CORES = 8, 2, 4, 2, 2
PLANE = ("lo", "x", "hi", "core")
NE = ROWS * XS
NK = HALVES * CORES
NV = 4
NO = 512
SLICES = NE * NK
DEPTH = 2 * NO // SLICES
HALO = 4
WIDE = NK * DEPTH


LOW, HIGH = 0, 1
DISTS = range(1, HALO + 1)


def mode_at(offsets, dist):
    mode = jnp.int32(0)
    for v in range(1, NV):
        mode = jnp.where(offsets[v] == dist, v, mode)
    return mode


def weight_kernel(offsets, occupation, weight, table, coupling, out, ordered, mixing):
    for k in range(NK):
        for q in range(NK):
            for v in range(NV):
                mixing[v, k, table[k, q]] = weight[q, v]
    row = lax.broadcasted_iota(jnp.int32, (DEPTH, WIDE), 0)
    column = lax.broadcasted_iota(jnp.int32, (DEPTH, WIDE), 1)
    for dist in DISTS:
        mode = mode_at(offsets, dist)
        ordered[dist - 1] = coupling[mode]
        for k in range(NK):
            base = jnp.zeros((DEPTH, WIDE), jnp.float32)
            for j in range(NK):
                base = jnp.where(column == row + DEPTH * j, mixing[mode, k, j], base)
            for side in (LOW, HIGH):
                scaled = base * (occupation[mode] + float(side))
                high = scaled.astype(jnp.bfloat16)
                rest = (scaled - high.astype(jnp.float32)).astype(jnp.bfloat16)
                columns = slice(side * WIDE, (side + 1) * WIDE)
                out[dist - 1, k * DEPTH : (k + 1) * DEPTH, columns] = high
                out[dist - 1, WIDE + k * DEPTH : WIDE + (k + 1) * DEPTH, columns] = rest


def block(ref, e):
    return ref[e * NK : (e + 1) * NK].reshape(WIDE, NO)


def store(out, dist, e, total):
    rounded = total.astype(jnp.bfloat16)
    for k in range(NK):
        out[e * NK + k, dist - 1] = rounded[k * DEPTH : (k + 1) * DEPTH]


def packed(dist):
    return dist * (dist - 1) // 2


def below_at(dist):
    return range(dist)


def above_at(dist):
    return range(NE - dist, NE)


def weighted(weights, source):
    total = jnp.dot(weights, source, preferred_element_type=jnp.float32)
    return total[:WIDE] + total[WIDE:]


def inner_kernel(scale, own, out, low_rest, high_rest):
    for dist in DISTS:
        weights = scale[dist - 1]
        for e in range(dist, NE - dist):
            both = jnp.concatenate([block(own, e - dist), block(own, e + dist)], axis=0)
            store(out, dist, e, weighted(weights, both))
        for index, e in enumerate(below_at(dist)):
            low_rest[packed(dist) + index] = weighted(weights[:, WIDE:], block(own, e + dist))
        for index, e in enumerate(above_at(dist)):
            high_rest[packed(dist) + index] = weighted(weights[:, :WIDE], block(own, e - dist))


def halo_kernel(side, scale, halo, rest, started, out):
    for reach in DISTS:
        source = HALO - reach if side == LOW else reach - 1
        columns = slice(side * WIDE, (side + 1) * WIDE)
        weights = scale[reach - 1 :, :, columns].reshape((HALO + 1 - reach) * 2 * WIDE, WIDE)
        total = jnp.dot(weights, block(halo, source), preferred_element_type=jnp.float32)
        for dist in range(reach, HALO + 1):
            index = dist - reach if side == LOW else reach - 1
            e = index if side == LOW else NE - dist + index
            first = (dist - reach) * 2 * WIDE
            part = total[first : first + WIDE] + total[first + WIDE : first + 2 * WIDE]
            store(out, dist, e, rest[packed(dist) + index] + part)


SMEM = pl.BlockSpec(memory_space=pltpu.SMEM)
VMEM = pl.BlockSpec(memory_space=pltpu.VMEM)
PARAMS = pltpu.CompilerParams(vmem_limit_bytes=18 << 20)
MIXED = jax.ShapeDtypeStruct((SLICES, NV, DEPTH, NO), jnp.bfloat16)
REST = jax.ShapeDtypeStruct((HALO * (HALO + 1) // 2, WIDE, NO), jnp.float32)


def by_distance(offsets, occupation, weight, table, coupling):
    return pl.pallas_call(
        weight_kernel,
        out_shape=[
            jax.ShapeDtypeStruct((HALO, 2 * WIDE, 2 * WIDE), jnp.bfloat16),
            jax.ShapeDtypeStruct((HALO, NO, NO), jnp.bfloat16),
        ],
        in_specs=[SMEM] * 4 + [VMEM],
        out_specs=[VMEM] * 2,
        scratch_shapes=[pltpu.SMEM((NV, NK, NK), jnp.float32)],
        compiler_params=PARAMS,
    )(offsets, occupation, weight, table, coupling)


def mixed_inner(scale, own):
    return pl.pallas_call(
        inner_kernel,
        out_shape=[MIXED, REST, REST],
        in_specs=[VMEM] * 2,
        out_specs=[VMEM] * 3,
        compiler_params=PARAMS,
    )(scale, own)


def mixed_side(side, scale, halo, rest, started):
    return pl.pallas_call(
        functools.partial(halo_kernel, side),
        out_shape=MIXED,
        in_specs=[VMEM] * 4,
        out_specs=VMEM,
        input_output_aliases={3: 0},
        compiler_params=PARAMS,
    )(scale, halo, rest, started)


def product_kernel(coupling, shifted, out):
    for part in range(2):
        total = None
        for v in range(NV):
            block = shifted[part * 16 : part * 16 + 16, v].reshape(NO, NO)
            left = jnp.dot(coupling[v], block, preferred_element_type=jnp.float32)
            term = lax.dot_general(
                left.astype(jnp.bfloat16),
                coupling[v],
                (((1,), (1,)), ((), ())),
                preferred_element_type=jnp.float32,
            )
            total = term if total is None else total + term
        out[part] = total.astype(jnp.bfloat16)


def products(coupling, shifted):
    vmem = pl.BlockSpec(memory_space=pltpu.VMEM)
    return pl.pallas_call(
        product_kernel,
        out_shape=jax.ShapeDtypeStruct((2, NO, NO), jnp.bfloat16),
        in_specs=[vmem] * 2,
        out_specs=vmem,
        compiler_params=pltpu.CompilerParams(vmem_limit_bytes=18 << 20),
    )(coupling, shifted)


def shards(green_lesser, coupling, offsets, occupation, transfer_weight, transfer_table):
    slices = green_lesser.reshape(SLICES, DEPTH, NO)
    own = lax.all_to_all(slices, PLANE, 0, 0, tiled=True)
    half = SLICES // 2
    below = lax.ppermute(own[half:], "z", [(z, z + 1) for z in range(PLANES - 1)])
    above = lax.ppermute(own[:half], "z", [(z + 1, z) for z in range(PLANES - 1)])
    scale, ordered = by_distance(offsets, occupation, transfer_weight, transfer_table, coupling)
    out, low_rest, high_rest = mixed_inner(scale, own)
    out = mixed_side(HIGH, scale, above, high_rest, out)
    out = mixed_side(LOW, scale, below, low_rest, out)
    shifted = lax.all_to_all(out.reshape(SLICES, NV * DEPTH, NO), PLANE, 0, 0, tiled=True)
    sigma = products(ordered, shifted.reshape(SLICES, NV, DEPTH, NO))
    return sigma[None, None]


def solution(mesh):
    fine = Mesh(
        mesh.devices.reshape(PLANES, ROWS, XS, HALVES, CORES),
        ("z", "lo", "x", "hi", "core"),
    )
    split = P(("z", "lo", "x"), ("hi", "core"), None, None, None)
    return jax.shard_map(
        shards,
        mesh=fine,
        in_specs=(split, P(), P(), P(), P(), P()),
        out_specs=split,
        check_vma=False,
    )
```

```python
import functools

import jax
import jax.numpy as jnp
from jax import lax
from jax.experimental import pallas as pl
from jax.experimental.pallas import tpu as pltpu
from jax.sharding import Mesh, PartitionSpec as P

PLANES, ROWS, XS, HALVES, CORES = 8, 2, 4, 2, 2
PLANE = ("lo", "x", "hi", "core")
NE = ROWS * XS
NK = HALVES * CORES
NV = 4
NO = 512
SLICES = NE * NK
DEPTH = 2 * NO // SLICES
HALO = 4
WIDE = NK * DEPTH


LOW, HIGH = 0, 1
DISTS = range(1, HALO + 1)


def mode_at(offsets, dist):
    mode = jnp.int32(0)
    for v in range(1, NV):
        mode = jnp.where(offsets[v] == dist, v, mode)
    return mode


def weight_kernel(offsets, occupation, weight, table, coupling, out, ordered, turned, mixing):
    for k in range(NK):
        for q in range(NK):
            for v in range(NV):
                mixing[v, k, table[k, q]] = weight[q, v]
    row = lax.broadcasted_iota(jnp.int32, (DEPTH, WIDE), 0)
    column = lax.broadcasted_iota(jnp.int32, (DEPTH, WIDE), 1)
    for dist in DISTS:
        mode = mode_at(offsets, dist)
        ordered[dist - 1] = coupling[mode]
        turned[dist - 1] = coupling[mode].T
        for k in range(NK):
            base = jnp.zeros((DEPTH, WIDE), jnp.float32)
            for j in range(NK):
                base = jnp.where(column == row + DEPTH * j, mixing[mode, k, j], base)
            for side in (LOW, HIGH):
                scaled = base * (occupation[mode] + float(side))
                high = scaled.astype(jnp.bfloat16)
                rest = (scaled - high.astype(jnp.float32)).astype(jnp.bfloat16)
                columns = slice(side * WIDE, (side + 1) * WIDE)
                out[dist - 1, k * DEPTH : (k + 1) * DEPTH, columns] = high
                out[dist - 1, WIDE + k * DEPTH : WIDE + (k + 1) * DEPTH, columns] = rest


def block(ref, e):
    return ref[e * NK : (e + 1) * NK].reshape(WIDE, NO)


def times_right(turned, dist, rows, energies, out):
    right = jnp.dot(rows, turned[dist - 1], preferred_element_type=jnp.float32)
    right = right.astype(jnp.bfloat16)
    for index, e in enumerate(energies):
        for k in range(NK):
            first = index * WIDE + k * DEPTH
            out[e * NK + k, dist - 1] = right[first : first + DEPTH]


def packed(dist):
    return dist * (dist - 1) // 2


def below_at(dist):
    return range(dist)


def above_at(dist):
    return range(NE - dist, NE)


def weighted(weights, source):
    total = jnp.dot(weights, source, preferred_element_type=jnp.float32)
    return total[:WIDE] + total[WIDE:]


def inner_kernel(scale, turned, own, out, low_rest, high_rest, sums):
    for dist in DISTS:
        weights = scale[dist - 1]
        energies = range(dist, NE - dist)
        for index, e in enumerate(energies):
            both = jnp.concatenate([block(own, e - dist), block(own, e + dist)], axis=0)
            sums[index] = weighted(weights, both).astype(jnp.bfloat16)
        if energies:
            rows = sums[0 : len(energies)].reshape(len(energies) * WIDE, NO)
            times_right(turned, dist, rows, energies, out)
        for index, e in enumerate(below_at(dist)):
            low_rest[packed(dist) + index] = weighted(weights[:, WIDE:], block(own, e + dist))
        for index, e in enumerate(above_at(dist)):
            high_rest[packed(dist) + index] = weighted(weights[:, :WIDE], block(own, e - dist))


def halo_kernel(side, scale, turned, halo, rest, started, out, sums):
    for reach in DISTS:
        source = HALO - reach if side == LOW else reach - 1
        columns = slice(side * WIDE, (side + 1) * WIDE)
        weights = scale[reach - 1 :, :, columns].reshape((HALO + 1 - reach) * 2 * WIDE, WIDE)
        total = jnp.dot(weights, block(halo, source), preferred_element_type=jnp.float32)
        for dist in range(reach, HALO + 1):
            index = packed(dist) + (dist - reach if side == LOW else reach - 1)
            first = (dist - reach) * 2 * WIDE
            part = total[first : first + WIDE] + total[first + WIDE : first + 2 * WIDE]
            sums[index] = (rest[index] + part).astype(jnp.bfloat16)
    for dist in DISTS:
        rows = sums[packed(dist) : packed(dist) + dist].reshape(dist * WIDE, NO)
        energies = below_at(dist) if side == LOW else above_at(dist)
        times_right(turned, dist, rows, energies, out)


SMEM = pl.BlockSpec(memory_space=pltpu.SMEM)
VMEM = pl.BlockSpec(memory_space=pltpu.VMEM)
PARAMS = pltpu.CompilerParams(vmem_limit_bytes=18 << 20)
MIXED = jax.ShapeDtypeStruct((SLICES, NV, DEPTH, NO), jnp.bfloat16)
REST = jax.ShapeDtypeStruct((HALO * (HALO + 1) // 2, WIDE, NO), jnp.float32)


def by_distance(offsets, occupation, weight, table, coupling):
    return pl.pallas_call(
        weight_kernel,
        out_shape=[
            jax.ShapeDtypeStruct((HALO, 2 * WIDE, 2 * WIDE), jnp.bfloat16),
            jax.ShapeDtypeStruct((HALO, NO, NO), jnp.bfloat16),
            jax.ShapeDtypeStruct((HALO, NO, NO), jnp.bfloat16),
        ],
        in_specs=[SMEM] * 4 + [VMEM],
        out_specs=[VMEM] * 3,
        scratch_shapes=[pltpu.SMEM((NV, NK, NK), jnp.float32)],
        compiler_params=PARAMS,
    )(offsets, occupation, weight, table, coupling)


def mixed_inner(scale, turned, own):
    return pl.pallas_call(
        inner_kernel,
        out_shape=[MIXED, REST, REST],
        in_specs=[VMEM] * 3,
        out_specs=[VMEM] * 3,
        scratch_shapes=[pltpu.VMEM((NE, WIDE, NO), jnp.bfloat16)],
        compiler_params=PARAMS,
    )(scale, turned, own)


def mixed_side(side, scale, turned, halo, rest, started):
    return pl.pallas_call(
        functools.partial(halo_kernel, side),
        out_shape=MIXED,
        in_specs=[VMEM] * 5,
        out_specs=VMEM,
        input_output_aliases={4: 0},
        scratch_shapes=[pltpu.VMEM(REST.shape, jnp.bfloat16)],
        compiler_params=PARAMS,
    )(scale, turned, halo, rest, started)


def product_kernel(ordered, right, out):
    half = SLICES // 2
    for part in range(2):
        total = None
        for index in range(HALO):
            rows = right[part * half : part * half + half, index].reshape(NO, NO)
            term = jnp.dot(ordered[index], rows, preferred_element_type=jnp.float32)
            total = term if total is None else total + term
        out[part] = total.astype(jnp.bfloat16)


def products(coupling, shifted):
    vmem = pl.BlockSpec(memory_space=pltpu.VMEM)
    return pl.pallas_call(
        product_kernel,
        out_shape=jax.ShapeDtypeStruct((2, NO, NO), jnp.bfloat16),
        in_specs=[vmem] * 2,
        out_specs=vmem,
        compiler_params=pltpu.CompilerParams(vmem_limit_bytes=18 << 20),
    )(coupling, shifted)


def shards(green_lesser, coupling, offsets, occupation, transfer_weight, transfer_table):
    slices = green_lesser.reshape(SLICES, DEPTH, NO)
    own = lax.all_to_all(slices, PLANE, 0, 0, tiled=True)
    half = SLICES // 2
    below = lax.ppermute(own[half:], "z", [(z, z + 1) for z in range(PLANES - 1)])
    above = lax.ppermute(own[:half], "z", [(z + 1, z) for z in range(PLANES - 1)])
    scale, ordered, turned = by_distance(offsets, occupation, transfer_weight, transfer_table, coupling)
    out, low_rest, high_rest = mixed_inner(scale, turned, own)
    out = mixed_side(HIGH, scale, turned, above, high_rest, out)
    out = mixed_side(LOW, scale, turned, below, low_rest, out)
    shifted = lax.all_to_all(out.reshape(SLICES, NV * DEPTH, NO), PLANE, 0, 0, tiled=True)
    sigma = products(ordered, shifted.reshape(SLICES, NV, DEPTH, NO))
    return sigma[None, None]


def solution(mesh):
    fine = Mesh(
        mesh.devices.reshape(PLANES, ROWS, XS, HALVES, CORES),
        ("z", "lo", "x", "hi", "core"),
    )
    split = P(("z", "lo", "x"), ("hi", "core"), None, None, None)
    return jax.shard_map(
        shards,
        mesh=fine,
        in_specs=(split, P(), P(), P(), P(), P()),
        out_specs=split,
        check_vma=False,
    )
```

```python
import functools

import jax
import jax.numpy as jnp
from jax import lax
from jax.experimental import pallas as pl
from jax.experimental.pallas import tpu as pltpu
from jax.sharding import Mesh, PartitionSpec as P

PLANES, ROWS, XS, HALVES, CORES = 8, 2, 4, 2, 2
PLANE = ("lo", "x", "hi", "core")
NE = ROWS * XS
NK = HALVES * CORES
NV = 4
NO = 512
SLICES = NE * NK
DEPTH = 2 * NO // SLICES
HALO = 4
WIDE = NK * DEPTH


LOW, HIGH = 0, 1
DISTS = range(1, HALO + 1)


def mode_at(offsets, dist):
    mode = jnp.int32(0)
    for v in range(1, NV):
        mode = jnp.where(offsets[v] == dist, v, mode)
    return mode


def weight_kernel(offsets, occupation, weight, table, coupling, out, ordered, turned, mixing):
    for k in range(NK):
        for q in range(NK):
            for v in range(NV):
                mixing[v, k, table[k, q]] = weight[q, v]
    row = lax.broadcasted_iota(jnp.int32, (DEPTH, WIDE), 0)
    column = lax.broadcasted_iota(jnp.int32, (DEPTH, WIDE), 1)
    for dist in DISTS:
        mode = mode_at(offsets, dist)
        ordered[dist - 1] = coupling[mode]
        turned[dist - 1] = coupling[mode].T
        for k in range(NK):
            base = jnp.zeros((DEPTH, WIDE), jnp.float32)
            for j in range(NK):
                base = jnp.where(column == row + DEPTH * j, mixing[mode, k, j], base)
            for side in (LOW, HIGH):
                scaled = base * (occupation[mode] + float(side))
                high = scaled.astype(jnp.bfloat16)
                rest = (scaled - high.astype(jnp.float32)).astype(jnp.bfloat16)
                columns = slice(side * WIDE, (side + 1) * WIDE)
                out[dist - 1, k * DEPTH : (k + 1) * DEPTH, columns] = high
                out[dist - 1, WIDE + k * DEPTH : WIDE + (k + 1) * DEPTH, columns] = rest


def block(ref, e):
    return ref[e * NK : (e + 1) * NK].reshape(WIDE, NO)


def times_right(turned, dist, rows, energies, out):
    right = jnp.dot(rows, turned[dist - 1], preferred_element_type=jnp.float32)
    right = right.astype(jnp.bfloat16)
    for index, e in enumerate(energies):
        for k in range(NK):
            first = index * WIDE + k * DEPTH
            out[e * NK + k, dist - 1] = right[first : first + DEPTH]


def packed(dist):
    return dist * (dist - 1) // 2


def below_at(dist):
    return range(dist)


def above_at(dist):
    return range(NE - dist, NE)


def weighted(weights, source):
    total = jnp.dot(weights, source, preferred_element_type=jnp.float32)
    return total[:WIDE] + total[WIDE:]


def inner_kernel(scale, turned, own, out, low_rest, high_rest, sums):
    for dist in DISTS:
        weights = scale[dist - 1]
        energies = range(dist, NE - dist)
        for index, e in enumerate(energies):
            both = jnp.concatenate([block(own, e - dist), block(own, e + dist)], axis=0)
            sums[index] = weighted(weights, both).astype(jnp.bfloat16)
        if energies:
            rows = sums[0 : len(energies)].reshape(len(energies) * WIDE, NO)
            times_right(turned, dist, rows, energies, out)
        for index, e in enumerate(below_at(dist)):
            low_rest[packed(dist) + index] = weighted(weights[:, WIDE:], block(own, e + dist))
        for index, e in enumerate(above_at(dist)):
            high_rest[packed(dist) + index] = weighted(weights[:, :WIDE], block(own, e - dist))


def halo_kernel(side, scale, turned, halo, rest, started, out, sums):
    for reach in DISTS:
        source = HALO - reach if side == LOW else reach - 1
        columns = slice(side * WIDE, (side + 1) * WIDE)
        weights = scale[reach - 1 :, :, columns].reshape((HALO + 1 - reach) * 2 * WIDE, WIDE)
        total = jnp.dot(weights, block(halo, source), preferred_element_type=jnp.float32)
        for dist in range(reach, HALO + 1):
            index = packed(dist) + (dist - reach if side == LOW else reach - 1)
            first = (dist - reach) * 2 * WIDE
            part = total[first : first + WIDE] + total[first + WIDE : first + 2 * WIDE]
            sums[index] = (rest[index] + part).astype(jnp.bfloat16)
    for dist in DISTS:
        rows = sums[packed(dist) : packed(dist) + dist].reshape(dist * WIDE, NO)
        energies = below_at(dist) if side == LOW else above_at(dist)
        times_right(turned, dist, rows, energies, out)


SMEM = pl.BlockSpec(memory_space=pltpu.SMEM)
VMEM = pl.BlockSpec(memory_space=pltpu.VMEM)
PARAMS = pltpu.CompilerParams(vmem_limit_bytes=18 << 20)
MIXED = jax.ShapeDtypeStruct((SLICES, NV, DEPTH, NO), jnp.bfloat16)
REST = jax.ShapeDtypeStruct((HALO * (HALO + 1) // 2, WIDE, NO), jnp.float32)


def by_distance(offsets, occupation, weight, table, coupling):
    return pl.pallas_call(
        weight_kernel,
        out_shape=[
            jax.ShapeDtypeStruct((HALO, 2 * WIDE, 2 * WIDE), jnp.bfloat16),
            jax.ShapeDtypeStruct((HALO, NO, NO), jnp.bfloat16),
            jax.ShapeDtypeStruct((HALO, NO, NO), jnp.bfloat16),
        ],
        in_specs=[SMEM] * 4 + [VMEM],
        out_specs=[VMEM] * 3,
        scratch_shapes=[pltpu.SMEM((NV, NK, NK), jnp.float32)],
        compiler_params=PARAMS,
    )(offsets, occupation, weight, table, coupling)


def mixed_inner(scale, turned, own):
    return pl.pallas_call(
        inner_kernel,
        out_shape=[MIXED, REST, REST],
        in_specs=[VMEM] * 3,
        out_specs=[VMEM] * 3,
        scratch_shapes=[pltpu.VMEM((NE, WIDE, NO), jnp.bfloat16)],
        compiler_params=PARAMS,
    )(scale, turned, own)


def mixed_side(side, scale, turned, halo, rest, started):
    return pl.pallas_call(
        functools.partial(halo_kernel, side),
        out_shape=MIXED,
        in_specs=[VMEM] * 5,
        out_specs=VMEM,
        input_output_aliases={4: 0},
        scratch_shapes=[pltpu.VMEM(REST.shape, jnp.bfloat16)],
        compiler_params=PARAMS,
    )(scale, turned, halo, rest, started)


def product_kernel(ordered, right, out, ready, sems):
    half = SLICES // 2
    copies = []
    for part in range(2):
        total = None
        for index in range(HALO):
            rows = right[part * half : part * half + half, index].reshape(NO, NO)
            term = jnp.dot(ordered[index], rows, preferred_element_type=jnp.float32)
            total = term if total is None else total + term
        ready[part] = total.astype(jnp.bfloat16)
        copy = pltpu.make_async_copy(ready.at[part], out.at[part], sems.at[part])
        copy.start()
        copies.append(copy)
    for copy in copies:
        copy.wait()


def products(ordered, right):
    return pl.pallas_call(
        product_kernel,
        out_shape=jax.ShapeDtypeStruct((2, NO, NO), jnp.bfloat16),
        in_specs=[VMEM] * 2,
        out_specs=pl.BlockSpec(memory_space=pl.ANY),
        scratch_shapes=[
            pltpu.VMEM((2, NO, NO), jnp.bfloat16),
            pltpu.SemaphoreType.DMA((2,)),
        ],
        compiler_params=PARAMS,
    )(ordered, right)


def shards(green_lesser, coupling, offsets, occupation, transfer_weight, transfer_table):
    slices = green_lesser.reshape(SLICES, DEPTH, NO)
    own = lax.all_to_all(slices, PLANE, 0, 0, tiled=True)
    half = SLICES // 2
    below = lax.ppermute(own[half:], "z", [(z, z + 1) for z in range(PLANES - 1)])
    above = lax.ppermute(own[:half], "z", [(z + 1, z) for z in range(PLANES - 1)])
    scale, ordered, turned = by_distance(offsets, occupation, transfer_weight, transfer_table, coupling)
    out, low_rest, high_rest = mixed_inner(scale, turned, own)
    out = mixed_side(HIGH, scale, turned, above, high_rest, out)
    out = mixed_side(LOW, scale, turned, below, low_rest, out)
    shifted = lax.all_to_all(out.reshape(SLICES, NV * DEPTH, NO), PLANE, 0, 0, tiled=True)
    sigma = products(ordered, shifted.reshape(SLICES, NV, DEPTH, NO))
    return sigma[None, None]


def solution(mesh):
    fine = Mesh(
        mesh.devices.reshape(PLANES, ROWS, XS, HALVES, CORES),
        ("z", "lo", "x", "hi", "core"),
    )
    split = P(("z", "lo", "x"), ("hi", "core"), None, None, None)
    return jax.shard_map(
        shards,
        mesh=fine,
        in_specs=(split, P(), P(), P(), P(), P()),
        out_specs=split,
        check_vma=False,
    )
```

```python
import functools

import jax
import jax.numpy as jnp
from jax import lax
from jax.experimental import pallas as pl
from jax.experimental.pallas import tpu as pltpu
from jax.sharding import Mesh, PartitionSpec as P

PLANES, ROWS, XS, HALVES, CORES = 8, 2, 4, 2, 2
PLANE = ("lo", "x", "hi", "core")
NE = ROWS * XS
NK = HALVES * CORES
NV = 4
NO = 512
SLICES = NE * NK
DEPTH = 2 * NO // SLICES
HALO = 4
WIDE = NK * DEPTH


LOW, HIGH = 0, 1
DISTS = range(1, HALO + 1)


def mode_at(offsets, dist):
    mode = jnp.int32(0)
    for v in range(1, NV):
        mode = jnp.where(offsets[v] == dist, v, mode)
    return mode


def weight_kernel(offsets, occupation, weight, table, coupling, out, ordered, turned, mixing):
    for k in range(NK):
        for q in range(NK):
            for v in range(NV):
                mixing[v, k, table[k, q]] = weight[q, v]
    row = lax.broadcasted_iota(jnp.int32, (DEPTH, WIDE), 0)
    column = lax.broadcasted_iota(jnp.int32, (DEPTH, WIDE), 1)
    for dist in DISTS:
        mode = mode_at(offsets, dist)
        ordered[dist - 1] = coupling[mode]
        turned[dist - 1] = coupling[mode].T
        for k in range(NK):
            base = jnp.zeros((DEPTH, WIDE), jnp.float32)
            for j in range(NK):
                base = jnp.where(column == row + DEPTH * j, mixing[mode, k, j], base)
            for side in (LOW, HIGH):
                scaled = base * (occupation[mode] + float(side))
                high = scaled.astype(jnp.bfloat16)
                rest = (scaled - high.astype(jnp.float32)).astype(jnp.bfloat16)
                rows = slice(k * DEPTH, (k + 1) * DEPTH)
                out[dist - 1, rows, 2 * side * WIDE : (2 * side + 1) * WIDE] = high
                out[dist - 1, rows, (2 * side + 1) * WIDE : (2 * side + 2) * WIDE] = rest


def block(ref, e):
    return ref[e * NK : (e + 1) * NK].reshape(WIDE, NO)


def times_right(turned, dist, rows, energies, out):
    right = jnp.dot(rows, turned[dist - 1], preferred_element_type=jnp.float32)
    right = right.astype(jnp.bfloat16)
    for index, e in enumerate(energies):
        for k in range(NK):
            first = index * WIDE + k * DEPTH
            out[e * NK + k, dist - 1] = right[first : first + DEPTH]


def packed(dist):
    return dist * (dist - 1) // 2


def below_at(dist):
    return range(dist)


def above_at(dist):
    return range(NE - dist, NE)


def weighted(weights, *sources):
    twice = jnp.concatenate([source for source in sources for _ in range(2)], axis=0)
    return jnp.dot(weights, twice, preferred_element_type=jnp.float32)


def inner_kernel(scale, turned, own, out, low_rest, high_rest, sums):
    for dist in DISTS:
        weights = scale[dist - 1]
        energies = range(dist, NE - dist)
        for index, e in enumerate(energies):
            total = weighted(weights, block(own, e - dist), block(own, e + dist))
            sums[index] = total.astype(jnp.bfloat16)
        if energies:
            rows = sums[0 : len(energies)].reshape(len(energies) * WIDE, NO)
            times_right(turned, dist, rows, energies, out)
        for index, e in enumerate(below_at(dist)):
            low_rest[packed(dist) + index] = weighted(weights[:, 2 * WIDE :], block(own, e + dist))
        for index, e in enumerate(above_at(dist)):
            high_rest[packed(dist) + index] = weighted(weights[:, : 2 * WIDE], block(own, e - dist))


def halo_kernel(side, scale, turned, halo, rest, started, out, sums):
    for reach in DISTS:
        source = HALO - reach if side == LOW else reach - 1
        columns = slice(2 * side * WIDE, (2 * side + 2) * WIDE)
        weights = scale[reach - 1 :, :, columns].reshape((HALO + 1 - reach) * WIDE, 2 * WIDE)
        total = weighted(weights, block(halo, source))
        for dist in range(reach, HALO + 1):
            index = packed(dist) + (dist - reach if side == LOW else reach - 1)
            first = (dist - reach) * WIDE
            part = total[first : first + WIDE]
            sums[index] = (rest[index] + part).astype(jnp.bfloat16)
    for dist in DISTS:
        rows = sums[packed(dist) : packed(dist) + dist].reshape(dist * WIDE, NO)
        energies = below_at(dist) if side == LOW else above_at(dist)
        times_right(turned, dist, rows, energies, out)


SMEM = pl.BlockSpec(memory_space=pltpu.SMEM)
VMEM = pl.BlockSpec(memory_space=pltpu.VMEM)
PARAMS = pltpu.CompilerParams(vmem_limit_bytes=18 << 20)
MIXED = jax.ShapeDtypeStruct((SLICES, NV, DEPTH, NO), jnp.bfloat16)
REST = jax.ShapeDtypeStruct((HALO * (HALO + 1) // 2, WIDE, NO), jnp.float32)


def by_distance(offsets, occupation, weight, table, coupling):
    return pl.pallas_call(
        weight_kernel,
        out_shape=[
            jax.ShapeDtypeStruct((HALO, WIDE, 4 * WIDE), jnp.bfloat16),
            jax.ShapeDtypeStruct((HALO, NO, NO), jnp.bfloat16),
            jax.ShapeDtypeStruct((HALO, NO, NO), jnp.bfloat16),
        ],
        in_specs=[SMEM] * 4 + [VMEM],
        out_specs=[VMEM] * 3,
        scratch_shapes=[pltpu.SMEM((NV, NK, NK), jnp.float32)],
        compiler_params=PARAMS,
    )(offsets, occupation, weight, table, coupling)


def mixed_inner(scale, turned, own):
    return pl.pallas_call(
        inner_kernel,
        out_shape=[MIXED, REST, REST],
        in_specs=[VMEM] * 3,
        out_specs=[VMEM] * 3,
        scratch_shapes=[pltpu.VMEM((NE, WIDE, NO), jnp.bfloat16)],
        compiler_params=PARAMS,
    )(scale, turned, own)


def mixed_side(side, scale, turned, halo, rest, started):
    return pl.pallas_call(
        functools.partial(halo_kernel, side),
        out_shape=MIXED,
        in_specs=[VMEM] * 5,
        out_specs=VMEM,
        input_output_aliases={4: 0},
        scratch_shapes=[pltpu.VMEM(REST.shape, jnp.bfloat16)],
        compiler_params=PARAMS,
    )(scale, turned, halo, rest, started)


def product_kernel(ordered, right, out, ready, sems):
    half = SLICES // 2
    copies = []
    for part in range(2):
        total = None
        for index in range(HALO):
            rows = right[part * half : part * half + half, index].reshape(NO, NO)
            term = jnp.dot(ordered[index], rows, preferred_element_type=jnp.float32)
            total = term if total is None else total + term
        ready[part] = total.astype(jnp.bfloat16)
        copy = pltpu.make_async_copy(ready.at[part], out.at[part], sems.at[part])
        copy.start()
        copies.append(copy)
    for copy in copies:
        copy.wait()


def products(ordered, right):
    return pl.pallas_call(
        product_kernel,
        out_shape=jax.ShapeDtypeStruct((2, NO, NO), jnp.bfloat16),
        in_specs=[VMEM] * 2,
        out_specs=pl.BlockSpec(memory_space=pl.ANY),
        scratch_shapes=[
            pltpu.VMEM((2, NO, NO), jnp.bfloat16),
            pltpu.SemaphoreType.DMA((2,)),
        ],
        compiler_params=PARAMS,
    )(ordered, right)


def shards(green_lesser, coupling, offsets, occupation, transfer_weight, transfer_table):
    slices = green_lesser.reshape(SLICES, DEPTH, NO)
    own = lax.all_to_all(slices, PLANE, 0, 0, tiled=True)
    half = SLICES // 2
    below = lax.ppermute(own[half:], "z", [(z, z + 1) for z in range(PLANES - 1)])
    above = lax.ppermute(own[:half], "z", [(z + 1, z) for z in range(PLANES - 1)])
    scale, ordered, turned = by_distance(offsets, occupation, transfer_weight, transfer_table, coupling)
    out, low_rest, high_rest = mixed_inner(scale, turned, own)
    out = mixed_side(HIGH, scale, turned, above, high_rest, out)
    out = mixed_side(LOW, scale, turned, below, low_rest, out)
    shifted = lax.all_to_all(out.reshape(SLICES, NV * DEPTH, NO), PLANE, 0, 0, tiled=True)
    sigma = products(ordered, shifted.reshape(SLICES, NV, DEPTH, NO))
    return sigma[None, None]


def solution(mesh):
    fine = Mesh(
        mesh.devices.reshape(PLANES, ROWS, XS, HALVES, CORES),
        ("z", "lo", "x", "hi", "core"),
    )
    split = P(("z", "lo", "x"), ("hi", "core"), None, None, None)
    return jax.shard_map(
        shards,
        mesh=fine,
        in_specs=(split, P(), P(), P(), P(), P()),
        out_specs=split,
        check_vma=False,
    )
```

```python
import functools

import jax
import jax.numpy as jnp
from jax import lax
from jax.experimental import pallas as pl
from jax.experimental.pallas import tpu as pltpu
from jax.sharding import Mesh, PartitionSpec as P

PLANES, ROWS, XS, HALVES, CORES = 8, 2, 4, 2, 2
PLANE = ("lo", "x", "hi", "core")
NE = ROWS * XS
NK = HALVES * CORES
NV = 4
NO = 512
SLICES = NE * NK
DEPTH = 2 * NO // SLICES
HALO = 4
WIDE = NK * DEPTH


LOW, HIGH = 0, 1
DISTS = range(1, HALO + 1)


def mode_at(offsets, dist):
    mode = jnp.int32(0)
    for v in range(1, NV):
        mode = jnp.where(offsets[v] == dist, v, mode)
    return mode


def weight_kernel(offsets, occupation, weight, table, coupling, out, ordered, turned, mixing):
    for k in range(NK):
        for q in range(NK):
            for v in range(NV):
                mixing[v, k, table[k, q]] = weight[q, v]
    row = lax.broadcasted_iota(jnp.int32, (DEPTH, WIDE), 0)
    column = lax.broadcasted_iota(jnp.int32, (DEPTH, WIDE), 1)
    for dist in DISTS:
        mode = mode_at(offsets, dist)
        ordered[dist - 1] = coupling[mode]
        turned[dist - 1] = coupling[mode].T
        for k in range(NK):
            base = jnp.zeros((DEPTH, WIDE), jnp.float32)
            for j in range(NK):
                base = jnp.where(column == row + DEPTH * j, mixing[mode, k, j], base)
            for side in (LOW, HIGH):
                scaled = base * (occupation[mode] + float(side))
                high = scaled.astype(jnp.bfloat16)
                rest = (scaled - high.astype(jnp.float32)).astype(jnp.bfloat16)
                rows = slice(k * DEPTH, (k + 1) * DEPTH)
                out[dist - 1, rows, 2 * side * WIDE : (2 * side + 1) * WIDE] = high
                out[dist - 1, rows, (2 * side + 1) * WIDE : (2 * side + 2) * WIDE] = rest


def block(ref, e):
    return ref[e * NK : (e + 1) * NK].reshape(WIDE, NO)


def times_right(turned, dist, rows, energies, out):
    right = jnp.dot(rows, turned[dist - 1], preferred_element_type=jnp.float32)
    right = right.astype(jnp.bfloat16)
    for index, e in enumerate(energies):
        for k in range(NK):
            first = index * WIDE + k * DEPTH
            out[e * NK + k, dist - 1] = right[first : first + DEPTH]


def packed(dist):
    return dist * (dist - 1) // 2


def below_at(dist):
    return range(dist)


def above_at(dist):
    return range(NE - dist, NE)


def weighted(weights, *sources):
    twice = jnp.concatenate([source for source in sources for _ in range(2)], axis=0)
    return jnp.dot(weights, twice, preferred_element_type=jnp.float32)


def inner_kernel(scale, turned, own, out, low_rest, high_rest, sums):
    for dist in DISTS:
        weights = scale[dist - 1]
        energies = range(dist, NE - dist)
        for index, e in enumerate(energies):
            total = weighted(weights, block(own, e - dist), block(own, e + dist))
            sums[index] = total.astype(jnp.bfloat16)
        if energies:
            rows = sums[0 : len(energies)].reshape(len(energies) * WIDE, NO)
            times_right(turned, dist, rows, energies, out)
        for index, e in enumerate(below_at(dist)):
            low_rest[packed(dist) + index] = weighted(weights[:, 2 * WIDE :], block(own, e + dist))
        for index, e in enumerate(above_at(dist)):
            high_rest[packed(dist) + index] = weighted(weights[:, : 2 * WIDE], block(own, e - dist))


def halo_kernel(side, scale, turned, halo, rest, started, out, sums):
    for reach in DISTS:
        source = HALO - reach if side == LOW else reach - 1
        columns = slice(2 * side * WIDE, (2 * side + 2) * WIDE)
        weights = scale[reach - 1 :, :, columns].reshape((HALO + 1 - reach) * WIDE, 2 * WIDE)
        total = weighted(weights, block(halo, source))
        for dist in range(reach, HALO + 1):
            index = packed(dist) + (dist - reach if side == LOW else reach - 1)
            first = (dist - reach) * WIDE
            part = total[first : first + WIDE]
            sums[index] = (rest[index] + part).astype(jnp.bfloat16)
    for dist in DISTS:
        rows = sums[packed(dist) : packed(dist) + dist].reshape(dist * WIDE, NO)
        energies = below_at(dist) if side == LOW else above_at(dist)
        times_right(turned, dist, rows, energies, out)


SMEM = pl.BlockSpec(memory_space=pltpu.SMEM)
VMEM = pl.BlockSpec(memory_space=pltpu.VMEM)
PARAMS = pltpu.CompilerParams(vmem_limit_bytes=18 << 20)
MIXED = jax.ShapeDtypeStruct((SLICES, NV, DEPTH, NO), jnp.bfloat16)
REST = jax.ShapeDtypeStruct((HALO * (HALO + 1) // 2, WIDE, NO), jnp.float32)


def by_distance(offsets, occupation, weight, table, coupling):
    return pl.pallas_call(
        weight_kernel,
        out_shape=[
            jax.ShapeDtypeStruct((HALO, WIDE, 4 * WIDE), jnp.bfloat16),
            jax.ShapeDtypeStruct((HALO, NO, NO), jnp.bfloat16),
            jax.ShapeDtypeStruct((HALO, NO, NO), jnp.bfloat16),
        ],
        in_specs=[SMEM] * 4 + [VMEM],
        out_specs=[VMEM] * 3,
        scratch_shapes=[pltpu.SMEM((NV, NK, NK), jnp.float32)],
        compiler_params=PARAMS,
    )(offsets, occupation, weight, table, coupling)


def mixed_inner(scale, turned, own):
    return pl.pallas_call(
        inner_kernel,
        out_shape=[MIXED, REST, REST],
        in_specs=[VMEM] * 3,
        out_specs=[VMEM] * 3,
        scratch_shapes=[pltpu.VMEM((NE, WIDE, NO), jnp.bfloat16)],
        compiler_params=PARAMS,
    )(scale, turned, own)


def mixed_side(side, scale, turned, halo, rest, started):
    return pl.pallas_call(
        functools.partial(halo_kernel, side),
        out_shape=MIXED,
        in_specs=[VMEM] * 5,
        out_specs=VMEM,
        input_output_aliases={4: 0},
        scratch_shapes=[pltpu.VMEM(REST.shape, jnp.bfloat16)],
        compiler_params=PARAMS,
    )(scale, turned, halo, rest, started)


def product_kernel(ordered, right, out, ready, sems):
    half = SLICES // 2
    copies = []
    for part in range(2):
        total = None
        for index in range(HALO):
            rows = right[part * half : part * half + half, index].reshape(NO, NO)
            term = jnp.dot(ordered[index], rows, preferred_element_type=jnp.float32)
            total = term if total is None else total + term
        for index in range(2):
            rows = slice(index * NO // 2, (index + 1) * NO // 2)
            ready[part, rows] = total[rows].astype(jnp.bfloat16)
            place = (part, pl.ds(index * NO // 2, NO // 2))
            copy = pltpu.make_async_copy(ready.at[place], out.at[place], sems.at[part, index])
            copy.start()
            copies.append(copy)
    for copy in copies:
        copy.wait()


def products(ordered, right):
    return pl.pallas_call(
        product_kernel,
        out_shape=jax.ShapeDtypeStruct((2, NO, NO), jnp.bfloat16),
        in_specs=[VMEM] * 2,
        out_specs=pl.BlockSpec(memory_space=pl.ANY),
        scratch_shapes=[
            pltpu.VMEM((2, NO, NO), jnp.bfloat16),
            pltpu.SemaphoreType.DMA((2, 2)),
        ],
        compiler_params=PARAMS,
    )(ordered, right)


def shards(green_lesser, coupling, offsets, occupation, transfer_weight, transfer_table):
    slices = green_lesser.reshape(SLICES, DEPTH, NO)
    own = lax.all_to_all(slices, PLANE, 0, 0, tiled=True)
    half = SLICES // 2
    below = lax.ppermute(own[half:], "z", [(z, z + 1) for z in range(PLANES - 1)])
    above = lax.ppermute(own[:half], "z", [(z + 1, z) for z in range(PLANES - 1)])
    scale, ordered, turned = by_distance(offsets, occupation, transfer_weight, transfer_table, coupling)
    out, low_rest, high_rest = mixed_inner(scale, turned, own)
    out = mixed_side(HIGH, scale, turned, above, high_rest, out)
    out = mixed_side(LOW, scale, turned, below, low_rest, out)
    shifted = lax.all_to_all(out.reshape(SLICES, NV * DEPTH, NO), PLANE, 0, 0, tiled=True)
    sigma = products(ordered, shifted.reshape(SLICES, NV, DEPTH, NO))
    return sigma[None, None]


def solution(mesh):
    fine = Mesh(
        mesh.devices.reshape(PLANES, ROWS, XS, HALVES, CORES),
        ("z", "lo", "x", "hi", "core"),
    )
    split = P(("z", "lo", "x"), ("hi", "core"), None, None, None)
    return jax.shard_map(
        shards,
        mesh=fine,
        in_specs=(split, P(), P(), P(), P(), P()),
        out_specs=split,
        check_vma=False,
    )
```
